32 devices in a mesh: grp: 2 (over x), res: 16 (over z, y, core).
Axes of the slice: x: 2, y: 2, z: 4, core: 2. Of those that a mesh axis runs over, the one named last changes fastest.
Arguments:
- alignment_activations: bfloat16 [128, 128, 256], P('grp', 'res'), parts along dimension 0, may hold values from -6 to 6
- projection_weight: bfloat16 [256, 64], replicated, may hold values from -0.375 to 0.375
- output_weight: bfloat16 [1024, 128], replicated, may hold values from -0.1875 to 0.1875
- output_bias: float32 [128], replicated, may hold values from -3 to 3
- pair_update_gradient: bfloat16 [256, 128, 128], P(('grp', 'res')), parts along dimension 0, may hold values from -6 to 6
- sequence_mask: int32 [128], P('grp'), parts along dimension 0, may hold values 0 or 1
- residue_mask: int32 [256], P('grp'), parts along dimension 0, may hold values 0 or 1
Outputs:
- pair_increment: bfloat16 [256, 128, 128], P(('grp', 'res')), parts along dimension 0
- alignment_gradient: bfloat16 [128, 128, 256], P('grp', 'res'), parts along dimension 0
The draws below stay inside these ranges and needn't reach their ends.
There are 2 independent parts, one for each index of `grp`. The reference program is written for one: setup_inputs(seed, part) draws one part's arguments, and reference() takes and returns one part's arrays. A program takes and returns all parts, laid end to end along the dimension named above; an argument that names none is the same for every part. Nothing has to cross between parts.
All inputs are finite; a program needn't handle non-finite values.
Results may differ from the reference program's by a relative error of at most 0.007.
Values may be sent and summed in bfloat16 or wider, within the bound.
A program may use at most 64 MiB of HBM per device.

```python
import jax
import jax.numpy as jnp
from jax import lax

ALIGNED_CHANNELS = 256
PROJECTED_WIDTH = 32
PAIR_WIDTH = 128
ALIGNED_SEQS = 64
RESIDUES_LOCAL = 8
RESIDUE_TOTAL = 128


def plant(drawn, own_key, low, largest):
    spot = [jax.random.randint(jax.random.fold_in(own_key, axis), (), 0, length) for axis, length in enumerate(drawn.shape)]
    widest = drawn.shape.index(max(drawn.shape))
    next_to = spot[:widest] + [(spot[widest] + 1) % drawn.shape[widest]] + spot[widest + 1:]
    return drawn.at[tuple(spot)].set(low).at[tuple(next_to)].set(largest)


def raised(drawn, stream_key, source, target, blocks, factor):
    def block_of(position):
        return (jnp.arange(drawn.shape[position]) // (drawn.shape[position] // blocks)).reshape((-1,) + (1,) * (drawn.ndim - 1 - position))

    first = jax.random.permutation(stream_key, blocks)[block_of(target)]
    second = (block_of(target) + blocks // 2) % blocks
    return jnp.where((block_of(source) == first) | (block_of(source) == second), factor * drawn, drawn)


def block_scale(own_key, shape, shards, smallest, high):
    level, own = 1.0, jax.random.fold_in(own_key, 6)
    for dim, parts in shards:
        steps = jnp.exp(jax.random.uniform(jax.random.fold_in(own, dim), (parts,), jnp.float32, smallest / len(shards), high / len(shards)))
        level = level * jnp.repeat(steps, shape[dim] // parts).reshape([-1 if axis == dim else 1 for axis in range(len(shape))])
    return level


def bell_draw(own_key, dims, deviation, reach, split=(), kind=jnp.bfloat16):
    factor_of = block_scale(own_key, dims, split, -0.22, 0.18) if split else 1.0
    drawn = jax.random.normal(own_key, dims, jnp.float32) * deviation * factor_of
    return jnp.minimum(jnp.maximum(drawn, -reach), reach).astype(kind)


def noise_with(stream_key, extent, scale, most, split, heavy, dtype=jnp.bfloat16):
    result = scale * jax.random.normal(stream_key, extent, jnp.float32)
    if split:
        result = result * block_scale(stream_key, extent, split, -0.22, 0.18)
    return jnp.clip(raised(result, jax.random.fold_in(stream_key, 3), *heavy), -most, most).astype(dtype)


def setup_inputs(seed: int = 0, part: int = 0) -> dict:
    arg_keys = jax.random.split(jax.random.key(seed), 8)
    part_splits = jax.random.split(jax.random.fold_in(arg_keys[7], part), 8)
    alignment_activations = bell_draw(part_splits[0], (ALIGNED_SEQS, RESIDUE_TOTAL, ALIGNED_CHANNELS), 1.0, 6.0, ((1, 16),))
    projection_weight = bell_draw(arg_keys[1], (ALIGNED_CHANNELS, 2 * PROJECTED_WIDTH), ALIGNED_CHANNELS ** -0.5, 0.375)
    output_weight = bell_draw(arg_keys[2], (PROJECTED_WIDTH * PROJECTED_WIDTH, PAIR_WIDTH), (PROJECTED_WIDTH * PROJECTED_WIDTH) ** -0.5, 0.1875)
    output_bias = bell_draw(arg_keys[3], (PAIR_WIDTH,), 0.5, 3.0, (), jnp.float32)
    pair_update_gradient = noise_with(part_splits[4], (RESIDUE_TOTAL, RESIDUE_TOTAL, PAIR_WIDTH), 1.0, 6.0, ((0, 16),), (0, 1, 16, 2.0))
    sequence_mask = plant((jax.random.randint(part_splits[5], (ALIGNED_SEQS,), 0, 4) < 3).astype(jnp.int32), jax.random.fold_in(part_splits[5], 1), 0, 1)
    residue_mask = plant((jax.random.randint(part_splits[6], (RESIDUE_TOTAL,), 0, 8) < 7).astype(jnp.int32), jax.random.fold_in(part_splits[6], 1), 0, 1)
    return dict(alignment_activations=alignment_activations, projection_weight=projection_weight, output_weight=output_weight, output_bias=output_bias, pair_update_gradient=pair_update_gradient, sequence_mask=sequence_mask, residue_mask=residue_mask)


eps_norm = 1e-05

def layer_norm_forward(values):
    mean_val = lax.optimization_barrier(jnp.mean(values, axis=-1, keepdims=True))
    centered = values - mean_val
    inverse_deviation = lax.rsqrt(lax.optimization_barrier(jnp.mean(centered * centered, axis=-1, keepdims=True)) + eps_norm)
    return (centered * inverse_deviation, inverse_deviation)

def layer_norm_backward(grad_out, scaled_product, inverse_deviation):
    mean_grad = lax.optimization_barrier(jnp.mean(grad_out, axis=-1, keepdims=True))
    mean_cross = lax.optimization_barrier(jnp.mean(grad_out * scaled_product, axis=-1, keepdims=True))
    return inverse_deviation * (grad_out - mean_grad - scaled_product * mean_cross)

def reference(alignment_activations, projection_weight, output_weight, output_bias, pair_update_gradient, sequence_mask, residue_mask):
    scaled_product, inverse_deviation = layer_norm_forward(alignment_activations.astype(jnp.float32))
    normalized_input = scaled_product.astype(jnp.bfloat16)
    residue_float_mask = residue_mask.astype(jnp.float32)
    alignment_mask = sequence_mask.astype(jnp.float32)[:, None] * residue_float_mask[None, :]
    projected_rows = jnp.dot(normalized_input.reshape(-1, ALIGNED_CHANNELS), projection_weight, preferred_element_type=jnp.float32)
    projected_rows = projected_rows.reshape(ALIGNED_SEQS, RESIDUE_TOTAL, 2 * PROJECTED_WIDTH) * alignment_mask[:, :, None]
    projected_rows = projected_rows.astype(jnp.bfloat16)
    left_projected = projected_rows[:, :, :PROJECTED_WIDTH]
    right_proj = projected_rows[:, :, PROJECTED_WIDTH:]
    live_rows = jnp.sum(sequence_mask.astype(jnp.float32))
    right_wide = right_proj.astype(jnp.float32)
    block_count = RESIDUE_TOTAL // RESIDUES_LOCAL
    left_pieces = left_projected.reshape(ALIGNED_SEQS, block_count, RESIDUES_LOCAL, PROJECTED_WIDTH).transpose(1, 0, 2, 3)
    cot_blocks = pair_update_gradient.reshape(block_count, RESIDUES_LOCAL, RESIDUE_TOTAL, PAIR_WIDTH)
    mask_blocks = residue_float_mask.reshape(block_count, RESIDUES_LOCAL)

    def step_block(right_gradient, inputs):
        left_blk, cot_blk, mask_blk = inputs
        pair_count = jnp.maximum(live_rows * mask_blk[:, None] * residue_float_mask[None, :], 1.0)
        left_wide = left_blk.astype(jnp.float32)
        outer = jnp.einsum('sic,sjd->ijcd', left_wide, right_wide).astype(jnp.bfloat16)
        update = jnp.dot(outer.reshape(-1, PROJECTED_WIDTH * PROJECTED_WIDTH), output_weight, preferred_element_type=jnp.float32)
        update = update.reshape(RESIDUES_LOCAL, RESIDUE_TOTAL, PAIR_WIDTH) + output_bias[None, None, :]
        update = (update / pair_count[:, :, None]).astype(jnp.bfloat16)
        grad_outer = jnp.dot(cot_blk.reshape(-1, PAIR_WIDTH), output_weight.T, preferred_element_type=jnp.float32)
        grad_outer = grad_outer.reshape(RESIDUES_LOCAL, RESIDUE_TOTAL, PROJECTED_WIDTH, PROJECTED_WIDTH) / pair_count[:, :, None, None]
        grad_outer = lax.optimization_barrier(grad_outer.astype(jnp.bfloat16)).astype(jnp.float32)
        left_gradient = jnp.einsum('ijcd,sjd->sic', grad_outer, right_wide)
        right_gradient = right_gradient + jnp.einsum('ijcd,sic->sjd', grad_outer, left_wide)
        return (right_gradient, (update, left_gradient))
    initial_gradient = jnp.zeros((ALIGNED_SEQS, RESIDUE_TOTAL, PROJECTED_WIDTH), jnp.float32)
    right_gradient, (updates, left_gradients) = lax.scan(step_block, initial_gradient, (left_pieces, cot_blocks, mask_blocks))
    pair_increment = updates.reshape(RESIDUE_TOTAL, RESIDUE_TOTAL, PAIR_WIDTH)
    left_gradient = left_gradients.transpose(1, 0, 2, 3).reshape(ALIGNED_SEQS, RESIDUE_TOTAL, PROJECTED_WIDTH)
    projection_gradient = jnp.concatenate([left_gradient, right_gradient], axis=-1) * alignment_mask[:, :, None]
    projection_gradient = projection_gradient.astype(jnp.bfloat16)
    normalized_gradient = jnp.dot(projection_gradient.reshape(-1, 2 * PROJECTED_WIDTH), projection_weight.T, preferred_element_type=jnp.float32)
    normalized_gradient = normalized_gradient.reshape(ALIGNED_SEQS, RESIDUE_TOTAL, ALIGNED_CHANNELS)
    alignment_gradient = layer_norm_backward(normalized_gradient, scaled_product, inverse_deviation).astype(jnp.bfloat16)
    return (pair_increment, alignment_gradient)
```

```python
import functools

import jax
import jax.numpy as jnp
from jax import lax
from jax.experimental import pallas as pl
from jax.experimental.pallas import tpu as pltpu
from jax.sharding import PartitionSpec as P

EPS = 1e-05
MESH = pl.DeviceIdType.MESH
F32 = jnp.float32
BF16 = jnp.bfloat16


def dot(a, b, ca, cb):
    return lax.dot_general(a, b, (((ca,), (cb,)), ((), ())), preferred_element_type=F32)


def kernel(
    n,
    x_ref,
    wp_ref,
    wo_ref,
    bias_ref,
    g_ref,
    seq_ref,
    res_ref,
    res_smem,
    upd_ref,
    out_ref,
    scaled_ref,
    inv_ref,
    wide_ref,
    wf_ref,
    w_ref,
    tr_ref,
    lw_ref,
    gm_ref,
    ra_ref,
    r_ref,
    rall_ref,
    part_ref,
    sib_ref,
    red_ref,
    rsin_ref,
    ag_send,
    ag_recv,
    fw_send,
    fw_recv,
    sib_sem,
    rs_send,
    rs_recv,
):
    S, L, C = x_ref.shape
    D = wp_ref.shape[1] // 2
    Q = wo_ref.shape[1]
    H = D // 2
    K = D * S
    R = g_ref.shape[1]
    nchip = n // 2
    me = lax.axis_index("res")
    kind = lax.rem(me, 2)
    chip = lax.div(me, 2)
    sibling = me + 1 - 2 * kind

    def peer(o):
        return lax.rem(chip + o, nchip) * 2 + kind

    def source(o):
        return lax.rem(chip + nchip - o, nchip)

    barrier = pltpu.get_barrier_semaphore()
    pl.semaphore_signal(barrier, inc=1, device_id={"res": sibling}, device_id_type=MESH)
    for o in range(1, nchip):
        pl.semaphore_signal(barrier, inc=1, device_id={"res": peer(o)}, device_id_type=MESH)

    seq_row = seq_ref[...].astype(F32)
    res_row = res_ref[...].astype(F32)
    live = jnp.sum(seq_row, axis=1, keepdims=True)
    same = lax.broadcasted_iota(jnp.int32, (S, S), 0) == lax.broadcasted_iota(jnp.int32, (S, S), 1)
    seq_col = jnp.sum(jnp.where(same, seq_row, 0.0), axis=1, keepdims=True)
    res_mine = [res_smem[me * L + j].astype(F32) for j in range(L)]

    x = x_ref[...].astype(F32).reshape(S * L, C)
    mean = jnp.mean(x, axis=1, keepdims=True)
    centered = x - mean
    inv = lax.rsqrt(jnp.mean(centered * centered, axis=1, keepdims=True) + EPS)
    scaled = centered * inv
    inv_ref[...] = jnp.broadcast_to(inv, inv_ref.shape)
    lanes = C // 2
    for h in range(2):
        scaled_ref[h] = scaled[:, h * lanes : (h + 1) * lanes]

    wp = wp_ref[...]
    w_left = wp[:, :D]
    wp_t = jnp.transpose(
        jnp.concatenate([wp.astype(F32), jnp.zeros((C, 128 - 2 * D), F32)], axis=1)
    ) if 2 * D < 128 else jnp.transpose(wp.astype(F32))
    wl_t = wp_t[:D].astype(BF16)
    wr_t = wp_t[D : 2 * D].astype(BF16)
    lefts = []
    for j in range(L):
        rows = jnp.concatenate(
            [scaled_ref[h, pl.ds(j, S, stride=L), :] for h in range(2)], axis=1
        )
        rows = (rows * (seq_col * res_mine[j])).astype(BF16)
        lefts.append(dot(rows, w_left, 1, 0).astype(BF16))
        twice = jnp.concatenate([rows, rows], axis=0)
        tr_ref[j * D : (j + 1) * D, :] = dot(wr_t, twice, 1, 1)
    left = jnp.concatenate(lefts, axis=0)
    first = lax.broadcasted_iota(jnp.int32, (L, 2 * S), 1) < S
    blocks = [
        jnp.where(first, tr_ref[pl.ds(v, L, stride=D), :], tr_ref[pl.ds(H + v, L, stride=D), :])
        for v in range(H)
    ]
    half = jnp.concatenate(blocks[: H // 2], axis=1), jnp.concatenate(blocks[H // 2 :], axis=1)
    rall_ref[kind, chip] = jnp.concatenate(half, axis=0).astype(BF16)

    pl.semaphore_wait(barrier, nchip)

    def gather(o):
        mine = rall_ref.at[kind, chip]
        return pltpu.make_async_remote_copy(
            mine, mine, ag_send.at[o], ag_recv.at[o], device_id={"res": peer(o)}, device_id_type=MESH
        )

    def gathered(o):
        got = rall_ref.at[kind, source(o)]
        return pltpu.make_async_remote_copy(
            got, got, ag_send.at[o], ag_recv.at[o], device_id={"res": peer(o)}, device_id_type=MESH
        )

    def forward(o):
        slab = rall_ref.at[kind, source(o)]
        return pltpu.make_async_remote_copy(
            slab, slab, fw_send.at[o], fw_recv.at[o], device_id={"res": sibling}, device_id_type=MESH
        )

    def forwarded(o):
        slab = rall_ref.at[1 - kind, source(o)]
        return pltpu.make_async_remote_copy(
            slab, slab, fw_send.at[o], fw_recv.at[o], device_id={"res": sibling}, device_id_type=MESH
        )

    for o in range(1, nchip):
        gather(o).start()
    forward(0).start()

    wf_ref[...] = wo_ref[...].astype(F32)
    for v in range(H):
        for e in range(2):
            w_ref[:, (2 * v + e) * Q : (2 * v + e + 1) * Q] = wf_ref[
                pl.ds(e * H + v, D, stride=D), :
            ].astype(BF16)
    for i in range(L):
        gm_ref[:, i * Q : (i + 1) * Q] = g_ref[i]

    for v in range(H):
        lw = dot(left, w_ref[:, 2 * v * Q : (2 * v + 2) * Q], 1, 0).astype(BF16)
        for e in range(2):
            for i in range(L):
                lw_ref[(2 * v + e) * S : (2 * v + e + 1) * S, i * Q : (i + 1) * Q] = lw[
                    i * S : (i + 1) * S, e * Q : (e + 1) * Q
                ]

    KH = K // 2
    step = 256
    for t in range(KH // step):
        pieces = [
            dot(gm_ref[...], lw_ref[h * KH + t * step : h * KH + (t + 1) * step, :], 1, 1).reshape(
                nchip, 2, L, step
            )
            for h in range(2)
        ]
        for kd in range(2):
            both = jnp.concatenate([pieces[0][:, kd], pieces[1][:, kd]], axis=1)
            part_ref[kd, :, :, t * step : (t + 1) * step] = both.astype(BF16)

    pair = pltpu.make_async_remote_copy(
        part_ref.at[1 - kind],
        sib_ref,
        sib_sem.at[0],
        sib_sem.at[1],
        device_id={"res": sibling},
        device_id_type=MESH,
    )
    pair.start()
    for o in range(1, nchip):
        gathered(o).wait_recv()
        forward(o).start()
    pair.wait_recv()
    red_ref[...] = (part_ref[kind].astype(F32) + sib_ref[...].astype(F32)).astype(BF16)

    def scatter(o):
        return pltpu.make_async_remote_copy(
            red_ref.at[lax.rem(chip + o, nchip)],
            rsin_ref.at[o],
            rs_send.at[o],
            rs_recv.at[o],
            device_id={"res": peer(o)},
            device_id_type=MESH,
        )

    for o in range(1, nchip):
        scatter(o).start()
    for o in range(nchip):
        forwarded(o).wait_recv()

    for h in range(2):
        kinds = [
            rall_ref[kd].astype(F32)[:, h * L : (h + 1) * L, :].reshape(nchip, 1, L, KH)
            for kd in range(2)
        ]
        ra_ref[:, h * KH : (h + 1) * KH] = (
            jnp.concatenate(kinds, axis=1).reshape(R, KH).astype(BF16)
        )

    for v in range(H):
        r = dot(ra_ref[:, v * 2 * S : (v + 1) * 2 * S], gm_ref[...], 0, 0).astype(BF16)
        for e in range(2):
            for i in range(L):
                r_ref[i * S : (i + 1) * S, (2 * v + e) * Q : (2 * v + e + 1) * Q] = r[
                    e * S : (e + 1) * S, i * Q : (i + 1) * Q
                ]
    left_grad = dot(r_ref[...], w_ref[...], 1, 1).astype(BF16)

    same_r = lax.broadcasted_iota(jnp.int32, (R, R), 0) == lax.broadcasted_iota(
        jnp.int32, (R, R), 1
    )
    res_col = jnp.sum(jnp.where(same_r, res_row, 0.0), axis=1, keepdims=True)
    live_col = live * res_col
    bias = bias_ref[...]
    for b in range(L // 2):
        u = dot(ra_ref[...], lw_ref[:, 2 * b * Q : (2 * b + 2) * Q], 1, 0)
        for e in range(2):
            i = 2 * b + e
            factor = 1.0 / jnp.maximum(live_col * res_mine[i], 1.0)
            upd_ref[i] = ((u[:, e * Q : (e + 1) * Q] + bias) * factor).astype(BF16)

    total = red_ref[chip].astype(F32)
    for o in range(1, nchip):
        scatter(o).wait_recv()
        total = total + rsin_ref[o].astype(F32)
    for v in range(H):
        h, u = v // (H // 2), v % (H // 2)
        tr_ref[pl.ds(v, L, stride=H), :] = total[h * L : (h + 1) * L, u * 2 * S : (u + 1) * 2 * S]

    inv_live = 1.0 / jnp.maximum(live, 1.0)
    seq_scale = seq_col * inv_live
    for j in range(L):
        piece = tr_ref[j * H : (j + 1) * H, :]
        right_t = jnp.concatenate([piece[:, :S], piece[:, S:]], axis=0).astype(BF16)
        gn = dot(left_grad[j * S : (j + 1) * S], wl_t, 1, 0) + dot(right_t, wr_t, 0, 0)
        gn = gn * (seq_scale * res_mine[j])
        for h in range(2):
            wide_ref[h, pl.ds(j, S, stride=L), :] = gn[:, h * lanes : (h + 1) * lanes]

    gn = jnp.concatenate([wide_ref[0], wide_ref[1]], axis=1)
    sc = jnp.concatenate([scaled_ref[0], scaled_ref[1]], axis=1)
    mean_g = jnp.mean(gn, axis=1, keepdims=True)
    mean_c = jnp.mean(gn * sc, axis=1, keepdims=True)
    result = inv_ref[:, :1] * (gn - mean_g - sc * mean_c)
    out_ref[...] = result.reshape(S, L, C).astype(BF16)

    for o in range(1, nchip):
        gather(o).wait_send()
        scatter(o).wait_send()
    for o in range(nchip):
        forward(o).wait_send()
    pair.wait_send()


def body(n, x, wp, wo, bias, g, seq, res):
    S, L, C = x.shape
    D = wp.shape[1] // 2
    Q = wo.shape[1]
    R = g.shape[1]
    K = D * S
    nchip = n // 2
    vm = pl.BlockSpec(memory_space=pltpu.VMEM)
    dma = pltpu.SemaphoreType.DMA
    slab = (2 * L, K // 2)
    return pl.pallas_call(
        functools.partial(kernel, n),
        out_shape=(
            jax.ShapeDtypeStruct((L, R, Q), BF16),
            jax.ShapeDtypeStruct((S, L, C), BF16),
        ),
        in_specs=[vm] * 7 + [pl.BlockSpec(memory_space=pltpu.SMEM)],
        out_specs=(vm, vm),
        scratch_shapes=[
            pltpu.VMEM((2, S * L, C // 2), F32),
            pltpu.VMEM((S * L, 128), F32),
            pltpu.VMEM((2, S * L, C // 2), F32),
            pltpu.VMEM((D * D, Q), F32),
            pltpu.VMEM((D, D * Q), BF16),
            pltpu.VMEM((L * D, 2 * S), F32),
            pltpu.VMEM((K, L * Q), BF16),
            pltpu.VMEM((R, L * Q), BF16),
            pltpu.VMEM((R, K), BF16),
            pltpu.VMEM((S * L, D * Q), BF16),
            pltpu.VMEM((2, nchip) + slab, BF16),
            pltpu.VMEM((2, nchip) + slab, BF16),
            pltpu.VMEM((nchip,) + slab, BF16),
            pltpu.VMEM((nchip,) + slab, BF16),
            pltpu.VMEM((nchip,) + slab, BF16),
            dma((nchip,)),
            dma((nchip,)),
            dma((nchip,)),
            dma((nchip,)),
            dma((2,)),
            dma((nchip,)),
            dma((nchip,)),
        ],
        compiler_params=pltpu.CompilerParams(
            collective_id=0, has_side_effects=True, vmem_limit_bytes=56 * 1024 * 1024
        ),
    )(x, wp, wo, bias.reshape(1, -1), g, seq.reshape(1, -1), res.reshape(1, -1), res)


def solution(mesh):
    in_specs = (
        P("grp", "res", None),
        P(),
        P(),
        P(),
        P(("grp", "res"), None, None),
        P("grp"),
        P("grp"),
    )
    out_specs = (P(("grp", "res"), None, None), P("grp", "res", None))
    return jax.shard_map(
        functools.partial(body, mesh.shape["res"]),
        mesh=mesh,
        in_specs=in_specs,
        out_specs=out_specs,
        check_vma=False,
    )
```

```python
import functools

import jax
import jax.numpy as jnp
from jax import lax
from jax.experimental import pallas as pl
from jax.experimental.pallas import tpu as pltpu
from jax.sharding import PartitionSpec as P

EPS = 1e-05
MESH = pl.DeviceIdType.MESH
F32 = jnp.float32
BF16 = jnp.bfloat16


def dot(a, b, ca, cb):
    return lax.dot_general(a, b, (((ca,), (cb,)), ((), ())), preferred_element_type=F32)


def kernel(
    n,
    x_ref,
    wp_ref,
    wo_hbm,
    bias_ref,
    g_hbm,
    seq_ref,
    res_ref,
    res_smem,
    upd_ref,
    scaled_ref,
    inv_ref,
    wide_ref,
    g_ref,
    wo_ref,
    wf_ref,
    w_ref,
    tr_ref,
    lw_ref,
    gm_ref,
    ra_ref,
    r_ref,
    rall_ref,
    part_ref,
    sib_ref,
    red_ref,
    rsin_ref,
    ag_send,
    ag_recv,
    fw_send,
    fw_recv,
    sib_sem,
    rs_send,
    rs_recv,
    in_sem,
):
    S, L, C = x_ref.shape
    D = wp_ref.shape[0] // 2
    Q = wo_ref.shape[1]
    H = D // 2
    K = D * S
    R = g_ref.shape[1]
    nchip = n // 2
    me = lax.axis_index("res")
    kind = lax.rem(me, 2)
    chip = lax.div(me, 2)
    sibling = me + 1 - 2 * kind

    def peer(o):
        return lax.rem(chip + o, nchip) * 2 + kind

    def source(o):
        return lax.rem(chip + nchip - o, nchip)

    load_w = pltpu.make_async_copy(wo_hbm, wo_ref, in_sem.at[0])
    load_g = pltpu.make_async_copy(g_hbm, g_ref, in_sem.at[1])
    load_w.start()
    load_g.start()

    barrier = pltpu.get_barrier_semaphore()
    pl.semaphore_signal(barrier, inc=1, device_id={"res": sibling}, device_id_type=MESH)
    for o in range(1, nchip):
        pl.semaphore_signal(barrier, inc=1, device_id={"res": peer(o)}, device_id_type=MESH)

    seq_row = seq_ref[...].astype(F32)
    res_row = res_ref[...].astype(F32)
    live = jnp.sum(seq_row, axis=1, keepdims=True)
    same = lax.broadcasted_iota(jnp.int32, (S, S), 0) == lax.broadcasted_iota(jnp.int32, (S, S), 1)
    seq_col = jnp.sum(jnp.where(same, seq_row, 0.0), axis=1, keepdims=True)
    res_mine = [res_smem[me * L + j].astype(F32) for j in range(L)]

    x = x_ref[...].astype(F32).reshape(S * L, C)
    mean = jnp.mean(x, axis=1, keepdims=True)
    centered = x - mean
    inv = lax.rsqrt(jnp.mean(centered * centered, axis=1, keepdims=True) + EPS)
    scaled = centered * inv
    inv_ref[...] = jnp.broadcast_to(inv, inv_ref.shape)
    lanes = C // 2
    for h in range(2):
        scaled_ref[h] = scaled[:, h * lanes : (h + 1) * lanes]

    wl_t = wp_ref[:D]
    wr_t = wp_ref[D:]
    lefts = []
    for j in range(L):
        rows = jnp.concatenate(
            [scaled_ref[h, pl.ds(j, S, stride=L), :] for h in range(2)], axis=1
        )
        rows = (rows * (seq_col * res_mine[j])).astype(BF16)
        lefts.append(dot(rows, wl_t, 1, 1).astype(BF16))
        twice = jnp.concatenate([rows, rows], axis=0)
        tr_ref[j * D : (j + 1) * D, :] = dot(wr_t, twice, 1, 1)
    left = jnp.concatenate(lefts, axis=0)
    first = lax.broadcasted_iota(jnp.int32, (L, 2 * S), 1) < S
    blocks = [
        jnp.where(first, tr_ref[pl.ds(v, L, stride=D), :], tr_ref[pl.ds(H + v, L, stride=D), :])
        for v in range(H)
    ]
    half = jnp.concatenate(blocks[: H // 2], axis=1), jnp.concatenate(blocks[H // 2 :], axis=1)
    rall_ref[kind, chip] = jnp.concatenate(half, axis=0).astype(BF16)

    pl.semaphore_wait(barrier, nchip)

    def gather(o):
        mine = rall_ref.at[kind, chip]
        return pltpu.make_async_remote_copy(
            mine, mine, ag_send.at[o], ag_recv.at[o], device_id={"res": peer(o)}, device_id_type=MESH
        )

    def gathered(o):
        got = rall_ref.at[kind, source(o)]
        return pltpu.make_async_remote_copy(
            got, got, ag_send.at[o], ag_recv.at[o], device_id={"res": peer(o)}, device_id_type=MESH
        )

    def forward(o):
        slab = rall_ref.at[kind, source(o)]
        return pltpu.make_async_remote_copy(
            slab, slab, fw_send.at[o], fw_recv.at[o], device_id={"res": sibling}, device_id_type=MESH
        )

    def forwarded(o):
        slab = rall_ref.at[1 - kind, source(o)]
        return pltpu.make_async_remote_copy(
            slab, slab, fw_send.at[o], fw_recv.at[o], device_id={"res": sibling}, device_id_type=MESH
        )

    for o in range(1, nchip):
        gather(o).start()
    forward(0).start()

    load_w.wait()
    wf_ref[...] = wo_ref[...].astype(F32)
    for v in range(H):
        for e in range(2):
            w_ref[:, (2 * v + e) * Q : (2 * v + e + 1) * Q] = wf_ref[
                pl.ds(e * H + v, D, stride=D), :
            ].astype(BF16)
    load_g.wait()
    for i in range(L):
        gm_ref[:, i * Q : (i + 1) * Q] = g_ref[i]

    for v in range(H):
        lw = dot(left, w_ref[:, 2 * v * Q : (2 * v + 2) * Q], 1, 0).astype(BF16)
        for e in range(2):
            for i in range(L):
                lw_ref[(2 * v + e) * S : (2 * v + e + 1) * S, i * Q : (i + 1) * Q] = lw[
                    i * S : (i + 1) * S, e * Q : (e + 1) * Q
                ]

    KH = K // 2
    step = 256
    for t in range(KH // step):
        pieces = [
            dot(gm_ref[...], lw_ref[h * KH + t * step : h * KH + (t + 1) * step, :], 1, 1).reshape(
                nchip, 2, L, step
            )
            for h in range(2)
        ]
        for kd in range(2):
            both = jnp.concatenate([pieces[0][:, kd], pieces[1][:, kd]], axis=1)
            part_ref[kd, :, :, t * step : (t + 1) * step] = both.astype(BF16)

    pair = pltpu.make_async_remote_copy(
        part_ref.at[1 - kind],
        sib_ref,
        sib_sem.at[0],
        sib_sem.at[1],
        device_id={"res": sibling},
        device_id_type=MESH,
    )
    pair.start()
    for o in range(1, nchip):
        gathered(o).wait_recv()
        forward(o).start()
    pair.wait_recv()
    red_ref[...] = (part_ref[kind].astype(F32) + sib_ref[...].astype(F32)).astype(BF16)

    def scatter(o):
        return pltpu.make_async_remote_copy(
            red_ref.at[lax.rem(chip + o, nchip)],
            rsin_ref.at[o],
            rs_send.at[o],
            rs_recv.at[o],
            device_id={"res": peer(o)},
            device_id_type=MESH,
        )

    for o in range(1, nchip):
        scatter(o).start()
    for o in range(nchip):
        forwarded(o).wait_recv()

    for h in range(2):
        kinds = [
            rall_ref[kd].astype(F32)[:, h * L : (h + 1) * L, :].reshape(nchip, 1, L, KH)
            for kd in range(2)
        ]
        ra_ref[:, h * KH : (h + 1) * KH] = (
            jnp.concatenate(kinds, axis=1).reshape(R, KH).astype(BF16)
        )

    for v in range(H):
        r = dot(ra_ref[:, v * 2 * S : (v + 1) * 2 * S], gm_ref[...], 0, 0).astype(BF16)
        for e in range(2):
            for i in range(L):
                r_ref[i * S : (i + 1) * S, (2 * v + e) * Q : (2 * v + e + 1) * Q] = r[
                    e * S : (e + 1) * S, i * Q : (i + 1) * Q
                ]
    left_grad = dot(r_ref[...], w_ref[...], 1, 1).astype(BF16)

    same_r = lax.broadcasted_iota(jnp.int32, (R, R), 0) == lax.broadcasted_iota(
        jnp.int32, (R, R), 1
    )
    res_col = jnp.sum(jnp.where(same_r, res_row, 0.0), axis=1, keepdims=True)
    live_col = live * res_col
    bias = bias_ref[...]
    for b in range(L // 2):
        u = dot(ra_ref[...], lw_ref[:, 2 * b * Q : (2 * b + 2) * Q], 1, 0)
        for e in range(2):
            i = 2 * b + e
            factor = 1.0 / jnp.maximum(live_col * res_mine[i], 1.0)
            upd_ref[i] = ((u[:, e * Q : (e + 1) * Q] + bias) * factor).astype(BF16)

    total = red_ref[chip].astype(F32)
    for o in range(1, nchip):
        scatter(o).wait_recv()
        total = total + rsin_ref[o].astype(F32)
    for v in range(H):
        h, u = v // (H // 2), v % (H // 2)
        tr_ref[pl.ds(v, L, stride=H), :] = total[h * L : (h + 1) * L, u * 2 * S : (u + 1) * 2 * S]

    inv_live = 1.0 / jnp.maximum(live, 1.0)
    seq_scale = seq_col * inv_live
    for j in range(L):
        piece = tr_ref[j * H : (j + 1) * H, :]
        right_t = jnp.concatenate([piece[:, :S], piece[:, S:]], axis=0).astype(BF16)
        gn = dot(left_grad[j * S : (j + 1) * S], wl_t, 1, 0) + dot(right_t, wr_t, 0, 0)
        gn = gn * (seq_scale * res_mine[j])
        for h in range(2):
            wide_ref[h, pl.ds(j, S, stride=L), :] = gn[:, h * lanes : (h + 1) * lanes]

    for o in range(1, nchip):
        gather(o).wait_send()
        scatter(o).wait_send()
    for o in range(nchip):
        forward(o).wait_send()
    pair.wait_send()


def finish(upd_ref, scaled_ref, inv_ref, wide_ref, upd_out, out_ref, sem):
    S, L, C = out_ref.shape
    copy = pltpu.make_async_copy(upd_ref, upd_out, sem.at[0])
    copy.start()
    gn = jnp.concatenate([wide_ref[0], wide_ref[1]], axis=1)
    sc = jnp.concatenate([scaled_ref[0], scaled_ref[1]], axis=1)
    mean_g = jnp.mean(gn, axis=1, keepdims=True)
    mean_c = jnp.mean(gn * sc, axis=1, keepdims=True)
    result = inv_ref[:, :1] * (gn - mean_g - sc * mean_c)
    out_ref[...] = result.reshape(S, L, C).astype(BF16)
    copy.wait()


def body(n, x, wp, wo, bias, g, seq, res):
    S, L, C = x.shape
    D = wp.shape[1] // 2
    hbm = pl.BlockSpec(memory_space=pl.ANY)
    Q = wo.shape[1]
    R = g.shape[1]
    K = D * S
    nchip = n // 2
    vm = pl.BlockSpec(memory_space=pltpu.VMEM)
    dma = pltpu.SemaphoreType.DMA
    slab = (2 * L, K // 2)
    upd, scaled, inv, wide = pl.pallas_call(
        functools.partial(kernel, n),
        out_shape=(
            pltpu.VMEM((L, R, Q), BF16),
            pltpu.VMEM((2, S * L, C // 2), F32),
            pltpu.VMEM((S * L, 128), F32),
            pltpu.VMEM((2, S * L, C // 2), F32),
        ),
        in_specs=[vm, vm, hbm, vm, hbm, vm, vm] + [pl.BlockSpec(memory_space=pltpu.SMEM)],
        out_specs=(vm, vm, vm, vm),
        scratch_shapes=[
            pltpu.VMEM((L, R, Q), BF16),
            pltpu.VMEM((D * D, Q), BF16),
            pltpu.VMEM((D * D, Q), F32),
            pltpu.VMEM((D, D * Q), BF16),
            pltpu.VMEM((L * D, 2 * S), F32),
            pltpu.VMEM((K, L * Q), BF16),
            pltpu.VMEM((R, L * Q), BF16),
            pltpu.VMEM((R, K), BF16),
            pltpu.VMEM((S * L, D * Q), BF16),
            pltpu.VMEM((2, nchip) + slab, BF16),
            pltpu.VMEM((2, nchip) + slab, BF16),
            pltpu.VMEM((nchip,) + slab, BF16),
            pltpu.VMEM((nchip,) + slab, BF16),
            pltpu.VMEM((nchip,) + slab, BF16),
            dma((nchip,)),
            dma((nchip,)),
            dma((nchip,)),
            dma((nchip,)),
            dma((2,)),
            dma((nchip,)),
            dma((nchip,)),
            dma((2,)),
        ],
        compiler_params=pltpu.CompilerParams(
            collective_id=0, has_side_effects=True, vmem_limit_bytes=60 * 1024 * 1024
        ),
    )(x, wp.T, wo, bias.reshape(1, -1), g, seq.reshape(1, -1), res.reshape(1, -1), res)
    return pl.pallas_call(
        finish,
        out_shape=(
            jax.ShapeDtypeStruct((L, R, Q), BF16),
            jax.ShapeDtypeStruct((S, L, C), BF16),
        ),
        in_specs=[vm] * 4,
        out_specs=(hbm, vm),
        scratch_shapes=[dma((1,))],
        compiler_params=pltpu.CompilerParams(vmem_limit_bytes=8 * 1024 * 1024),
    )(upd, scaled, inv, wide)


def solution(mesh):
    in_specs = (
        P("grp", "res", None),
        P(),
        P(),
        P(),
        P(("grp", "res"), None, None),
        P("grp"),
        P("grp"),
    )
    out_specs = (P(("grp", "res"), None, None), P("grp", "res", None))
    return jax.shard_map(
        functools.partial(body, mesh.shape["res"]),
        mesh=mesh,
        in_specs=in_specs,
        out_specs=out_specs,
        check_vma=False,
    )
```
